256 devices in a mesh: sx: 32 (over x, z_lo, core), sy: 8 (over z_hi, y).
Axes of the slice: x: 4, y: 4, z: 8 (z_hi: 2, z_lo: 4; z = z_hi * 4 + z_lo), core: 2. Of those that a mesh axis runs over, the one named last changes fastest.
Arguments:
- queries: bfloat16 [128, 5120], P('sx'), may hold values from -120 to 120
- cached_key_rows: bfloat16 [524288, 1024], P(('sx', 'sy')), may hold values from -6 to 6
- cached_value_rows: bfloat16 [524288, 1024], P(('sx', 'sy')), may hold values from -6 to 6
- stretch_opening_index: int32 [1], replicated, may hold values from 516096 to 524160
- valid_lengths: int32 [256], P(('sx', 'sy')), may hold values from 1024 to 2048, as said below
- out_weight: bfloat16 [5120, 5120], P('sy', 'sx'), may hold values from -0.078125 to 0.078125
Outputs:
- output: bfloat16 [128, 5120], P('sy', 'sx')
The draws below stay inside these ranges and needn't reach their ends.
Inputs may be any that keep to these rules, and one draw needn't show every extreme that they name: `valid_lengths`: some block is full in every draw.
All inputs are finite; a program needn't handle non-finite values.
Results may differ from the reference program's by a relative error of at most 0.0049.
Values may be sent and summed in bfloat16 or wider, within the bound.
No kernel may reach another device: no remote copies, remote signals or barrier semaphores. Data moves between devices by JAX's collectives and lax.ppermute only.
A program may use at most 128 MiB of HBM per device.

```python
import jax
import jax.numpy as jnp
from jax import lax

D = 5120
HQ = 40
KEY_VALUE_HEADS = 8
HEAD_SIZE = 128
QUERY_GROUP_SIZE = 5
SPAN_TOKENS = 128
CACHE_PER_DEVICE = 2048
CACHE_POSITIONS = 524288


def draw_cached_key_rows(key, part):
    key = jax.random.fold_in(key, 3)
    base_position = jnp.clip(jax.random.normal(key, (CACHE_POSITIONS, KEY_VALUE_HEADS * HEAD_SIZE), jnp.float32), -6.0, 6.0)
    return base_position.astype(jnp.bfloat16)


def draw_queries(key, part):
    key = jax.random.fold_in(key, 4)
    base_position = 3.0 * jnp.clip(jax.random.normal(key, (SPAN_TOKENS, HQ * HEAD_SIZE), jnp.float32), -6.0, 6.0)
    return base_position.astype(jnp.bfloat16)


def draw_valid_lengths(key, part):
    key = jax.random.fold_in(key, 5)
    count_of_blocks = CACHE_POSITIONS // CACHE_PER_DEVICE
    lengths = jax.random.randint(key, (count_of_blocks,), CACHE_PER_DEVICE // 2, CACHE_PER_DEVICE + 1)
    full_block = jax.random.randint(jax.random.fold_in(key, 6), (), 0, count_of_blocks)
    return lengths.at[full_block].set(CACHE_PER_DEVICE).astype(jnp.int32)


def shard_levels(stream_key, shape, split, least, high):
    def one(position, shards_of):
        heights = jax.random.uniform(jax.random.fold_in(jax.random.fold_in(stream_key, 6), position), (shards_of,), jnp.float32, least / len(split), high / len(split))
        return jnp.repeat(jnp.exp(heights), shape[position] // shards_of).reshape((-1,) + (1,) * (len(shape) - position - 1))

    factor_of = one(*split[0])
    for cut in split[1:]:
        factor_of = factor_of * one(*cut)
    return factor_of


def centred(rng, dims, width, most, cuts=(), kind=jnp.bfloat16):
    drawn = jax.random.normal(rng, dims, jnp.float32) * width
    if len(cuts) > 0:
        drawn = shard_levels(rng, dims, cuts, -0.22, 0.18) * drawn
    return jnp.clip(drawn, min=-most, max=most).astype(kind)


def setup_inputs(seed: int = 0) -> dict:
    key_of = jax.random.split(jax.random.key(seed), 7)
    queries = draw_queries(jax.random.fold_in(key_of[6], 71), 0)
    cached_key_rows = draw_cached_key_rows(jax.random.fold_in(key_of[6], 71), 0)
    cached_value_rows = centred(key_of[2], (CACHE_POSITIONS, KEY_VALUE_HEADS * HEAD_SIZE), 1.0, 6.0, ((0, 256),))
    stretch_opening_index = jax.random.randint(key_of[3], (1,), CACHE_POSITIONS - 4 * CACHE_PER_DEVICE, CACHE_POSITIONS - SPAN_TOKENS + 1).astype(jnp.int32)
    valid_lengths = draw_valid_lengths(jax.random.fold_in(key_of[6], 71), 0)
    out_weight = centred(key_of[5], (HQ * HEAD_SIZE, D), (HQ * HEAD_SIZE) ** -0.5, 0.078125, ((0, 8), (1, 32)))
    return {"queries": queries, "cached_key_rows": cached_key_rows, "cached_value_rows": cached_value_rows, "stretch_opening_index": stretch_opening_index, "valid_lengths": valid_lengths, "out_weight": out_weight}


def normalizer_divisor(stretch_opening_index):
    positions = stretch_opening_index[0] + jnp.arange(SPAN_TOKENS, dtype=jnp.int32)
    buckets = ((positions + 1) // 8192).astype(jnp.float32)
    return (1.0 + 0.1 * jnp.log(buckets + 1.0)) * (HEAD_SIZE ** -0.5)


def reference(queries, cached_key_rows, cached_value_rows, stretch_opening_index, valid_lengths, out_weight):
    count_of_blocks = CACHE_POSITIONS // CACHE_PER_DEVICE
    heads_of_query = queries.astype(jnp.float32).reshape(SPAN_TOKENS, KEY_VALUE_HEADS, QUERY_GROUP_SIZE, HEAD_SIZE)
    score_multiplier = normalizer_divisor(stretch_opening_index)
    query_positions = stretch_opening_index[0] + jnp.arange(SPAN_TOKENS, dtype=jnp.int32)
    blocked_keys = cached_key_rows.reshape(count_of_blocks, CACHE_PER_DEVICE, KEY_VALUE_HEADS, HEAD_SIZE)
    blocked_values = cached_value_rows.reshape(count_of_blocks, CACHE_PER_DEVICE, KEY_VALUE_HEADS, HEAD_SIZE)
    block_ids = jnp.arange(count_of_blocks, dtype=jnp.int32)

    def visit(carry, inputs):
        running_max, running_out, running_total = carry
        key_block, value_block, extent_along, block_id = inputs
        scores = jnp.einsum("tgid,cgd->tgic", heads_of_query, key_block.astype(jnp.float32))
        scores = scores * score_multiplier[:, None, None, None]
        entry_indices = jnp.arange(CACHE_PER_DEVICE, dtype=jnp.int32)
        key_positions = block_id * CACHE_PER_DEVICE + entry_indices
        visible = (entry_indices < extent_along)[None, :] & (key_positions[None, :] <= query_positions[:, None])
        seen_mask = visible[:, None, None, :]
        scores = jnp.where(seen_mask, scores, -1e30)
        block_max = jnp.max(scores, axis=-1)
        weights = jnp.where(seen_mask, jnp.exp(scores - block_max[..., None]), 0.0)
        block_total = jnp.sum(weights, axis=-1)
        rounded = lax.optimization_barrier(weights.astype(jnp.bfloat16))
        block_out = jnp.einsum("tgic,cgd->tgid", rounded.astype(jnp.float32), value_block.astype(jnp.float32))
        updated_peak = jnp.maximum(running_max, block_max)
        old_factor = jnp.exp(running_max - updated_peak)
        new_factor = jnp.exp(block_max - updated_peak)
        running_out = running_out * old_factor[..., None] + block_out * new_factor[..., None]
        running_total = running_total * old_factor + block_total * new_factor
        return (updated_peak, running_out, running_total), None

    initial_state = (jnp.full((SPAN_TOKENS, KEY_VALUE_HEADS, QUERY_GROUP_SIZE), -1e30, jnp.float32),
                   jnp.zeros((SPAN_TOKENS, KEY_VALUE_HEADS, QUERY_GROUP_SIZE, HEAD_SIZE), jnp.float32),
                   jnp.zeros((SPAN_TOKENS, KEY_VALUE_HEADS, QUERY_GROUP_SIZE), jnp.float32))
    final_carry, unused = lax.scan(visit, initial_state, (blocked_keys, blocked_values, valid_lengths, block_ids))
    summed = final_carry[1]
    total = final_carry[2]
    attended = (summed / total[..., None]).reshape(SPAN_TOKENS, HQ * HEAD_SIZE).astype(jnp.bfloat16)
    return jnp.dot(attended, out_weight, preferred_element_type=jnp.float32).astype(jnp.bfloat16)
```

```python
import functools

import jax
import jax.numpy as jnp
from jax import lax
from jax.experimental import pallas as pl
from jax.experimental.pallas import tpu as pltpu
from jax.sharding import PartitionSpec as P

HQ = 40
KEY_VALUE_HEADS = 8
HEAD_SIZE = 128
GROUP = 5
LOG2E = 1.4426950408889634
BF16 = jnp.bfloat16
F32 = jnp.float32
CHIPS = 16
Y = 4
CORE_HEADS = 4
CHUNK = 1024


def attention_kernel(
    info, queries, key_own, key_pair, value_own, value_pair, scale, out, stats, bias, lhs
):
    head = pl.program_id(0)
    tokens = queries.shape[0]
    slots = key_own.shape[0]
    rows = tokens * GROUP

    @pl.when(head == 0)
    def _():
        step = 512

        def fill(i, carry):
            start = i * step
            place = lax.broadcasted_iota(jnp.int32, (step, tokens), 0) + start
            token = lax.broadcasted_iota(jnp.int32, (step, tokens), 1)
            pair = place >= slots
            entry = jnp.where(pair, place - slots, place)
            limit = jnp.where(pair, info[2], info[1])
            base = jnp.where(pair, info[4], info[3])
            seen = (entry < limit) & (base + entry <= token)
            bias[pl.ds(pl.multiple_of(start, step), step), :] = jnp.where(seen, 0.0, -1e30).astype(BF16)
            return carry

        lax.fori_loop(0, 2 * slots // step, fill, 0)

    one_hot = (
        lax.broadcasted_iota(jnp.int32, (tokens, tokens), 0)
        == lax.broadcasted_iota(jnp.int32, (tokens, tokens), 1)
    ).astype(BF16)
    for g in range(GROUP):
        lhs[g * tokens : (g + 1) * tokens, :HEAD_SIZE] = queries[:, g * HEAD_SIZE : (g + 1) * HEAD_SIZE]
        lhs[g * tokens : (g + 1) * tokens, HEAD_SIZE:] = one_hot
    left = lhs[...]
    factor = jnp.concatenate([scale[...]] * GROUP, axis=0)[:, :1]
    peak = None
    for source, (keys, values) in enumerate(((key_own, value_own), (key_pair, value_pair))):
        for start in range(0, slots, CHUNK):
            at = slice(source * slots + start, source * slots + start + CHUNK)
            right = jnp.concatenate([keys[start : start + CHUNK, :], bias[at, :]], axis=1)
            scores = lax.dot_general(
                left, right, (((1,), (1,)), ((), ())), preferred_element_type=F32
            )
            top = jnp.max(scores, axis=1, keepdims=True)
            new_peak = top if peak is None else jnp.maximum(peak, top)
            weights = jnp.exp2((scores - new_peak) * factor).astype(BF16)
            both = jnp.concatenate(
                [values[start : start + CHUNK, :], jnp.ones((CHUNK, HEAD_SIZE), BF16)], axis=1
            )
            part = jnp.dot(weights, both, preferred_element_type=F32)
            total = part if peak is None else total * jnp.exp2((peak - new_peak) * factor) + part
            peak = new_peak
    out[0] = total[:, :HEAD_SIZE].astype(BF16)
    lane = lax.broadcasted_iota(jnp.int32, (rows, HEAD_SIZE), 1)
    rest_m = jnp.broadcast_to(peak * factor, (rows, HEAD_SIZE))
    rest_l = total[:, HEAD_SIZE:]
    packed = jnp.zeros((rows, HEAD_SIZE), F32)
    for k in range(3):
        term_m = rest_m.astype(BF16).astype(F32)
        term_l = rest_l.astype(BF16).astype(F32)
        packed = jnp.where(lane == k, term_m, jnp.where(lane == 3 + k, term_l, packed))
        rest_m, rest_l = rest_m - term_m, rest_l - term_l
    stats[0] = packed.astype(BF16)


def attend(info, queries, keys, values, key_pair, value_pair, scale):
    tokens = queries.shape[0]
    slots = keys.shape[0]
    rows = tokens * GROUP
    own = pl.BlockSpec((slots, HEAD_SIZE), lambda h, s: (0, s[0] * CORE_HEADS + h))
    pair = pl.BlockSpec((slots, HEAD_SIZE), lambda h, s: (0, h))
    result = pl.BlockSpec((1, rows, HEAD_SIZE), lambda h, s: (h, 0, 0))
    return pl.pallas_call(
        attention_kernel,
        grid_spec=pltpu.PrefetchScalarGridSpec(
            num_scalar_prefetch=1,
            grid=(CORE_HEADS,),
            in_specs=[
                pl.BlockSpec((tokens, GROUP * HEAD_SIZE), lambda h, s: (0, h)),
                own,
                pair,
                own,
                pair,
                pl.BlockSpec((tokens, HEAD_SIZE), lambda h, s: (0, 0)),
            ],
            out_specs=[result, result],
            scratch_shapes=[
                pltpu.VMEM((2 * slots, tokens), BF16),
                pltpu.VMEM((rows, 2 * HEAD_SIZE), BF16),
            ],
        ),
        out_shape=[jax.ShapeDtypeStruct((CORE_HEADS, rows, HEAD_SIZE), BF16)] * 2,
        compiler_params=pltpu.CompilerParams(vmem_limit_bytes=60 * 2**20),
        cost_estimate=pl.CostEstimate(
            flops=2 * 2 * CORE_HEADS * rows * 2 * slots * 2 * HEAD_SIZE,
            bytes_accessed=2 * 2 * CORE_HEADS * 2 * slots * HEAD_SIZE,
            transcendentals=CORE_HEADS * rows * 2 * slots,
        ),
    )(info, queries, keys, key_pair, values, value_pair, scale)


def per_device(queries, keys, values, opening, valid, weight):
    sx, sy = lax.axis_index("sx"), lax.axis_index("sy")
    size_x, size_y = lax.axis_size("sx"), lax.axis_size("sy")
    core = sx % 2
    own_rows = queries.shape[0]
    tokens = own_rows * size_x
    slots = keys.shape[0]
    half = CORE_HEADS * GROUP * HEAD_SIZE
    kv_half = CORE_HEADS * HEAD_SIZE
    other_core = [(i, i ^ 1) for i in range(size_x)]

    def halves(a, width):
        mine = lax.dynamic_slice_in_dim(a, core * width, width, 1)
        return mine, lax.dynamic_slice_in_dim(a, (1 - core) * width, width, 1)

    mine, theirs = halves(queries, half)
    got = lax.ppermute(theirs, "sx", other_core)
    chip_rows = jnp.concatenate(
        [jnp.where(core == 0, mine, got), jnp.where(core == 0, got, mine)], axis=0
    )
    core_groups = [[i * 2 + c for i in range(CHIPS)] for c in range(2)]
    all_queries = lax.all_to_all(
        jnp.broadcast_to(chip_rows[None], (CHIPS, 2 * own_rows, half)),
        "sx", 0, 0, tiled=True, axis_index_groups=core_groups,
    ).reshape(tokens, half)

    key_pair = lax.ppermute(halves(keys, kv_half)[1], "sx", other_core)
    value_pair = lax.ppermute(halves(values, kv_half)[1], "sx", other_core)
    valid_pair = lax.ppermute(valid, "sx", other_core)

    far = lax.ppermute(weight, "sy", [(i, i ^ Y) for i in range(size_y)])
    near = jnp.stack([weight, far])
    blocks = [near] + [lax.ppermute(near, "sy", [(i, i ^ k) for i in range(size_y)]) for k in (1, 2, 3)]

    base = (sx * size_y + sy) * slots - opening[0]
    base_pair = ((sx ^ 1) * size_y + sy) * slots - opening[0]
    info = jnp.stack([core, valid[0], valid_pair[0], base, base_pair]).astype(jnp.int32)
    positions = opening[0] + jnp.arange(tokens, dtype=jnp.int32)
    buckets = ((positions + 1) // 8192).astype(F32)
    temper = (1.0 + 0.1 * jnp.log(buckets + 1.0)) * HEAD_SIZE ** (-0.5)
    scale = jnp.broadcast_to((temper * LOG2E)[:, None], (tokens, HEAD_SIZE))
    out, stats = attend(info, all_queries, keys, values, key_pair, value_pair, scale)

    z_lo = CHIPS // CORE_HEADS
    sub = tokens // size_y // z_lo
    piece_rows = GROUP * sub
    pieces = out.reshape(CORE_HEADS, GROUP, size_y, z_lo, sub, HEAD_SIZE).transpose(0, 3, 2, 1, 4, 5)
    pieces = pieces.reshape(CHIPS * size_y, piece_rows, HEAD_SIZE)
    extra = stats[..., :6].reshape(CORE_HEADS, GROUP, size_y, z_lo, sub, 6).transpose(0, 3, 2, 5, 1, 4)
    extra = extra.reshape(CHIPS * size_y, 1, 6 * piece_rows)
    extra = jnp.pad(extra, ((0, 0), (0, 0), (0, HEAD_SIZE - 6 * piece_rows)))
    all_groups = [
        [(i * 2 + c) * size_y + j for i in range(CHIPS) for j in range(size_y)] for c in range(2)
    ]
    received = lax.all_to_all(
        jnp.concatenate([pieces, extra], axis=1),
        ("sx", "sy"), 0, 0, tiled=True, axis_index_groups=all_groups,
    )
    terms = received[:, piece_rows, : 6 * piece_rows].astype(F32).reshape(-1, 2, 3, piece_rows)
    terms = terms[:, :, 0] + (terms[:, :, 1] + terms[:, :, 2])
    peak, total = terms[:, 0], terms[:, 1]
    share = jnp.exp2(peak - jnp.max(peak, axis=0))
    summed = jnp.sum(received[:, :piece_rows].astype(F32) * share[..., None], axis=0)
    attended = (summed / jnp.sum(share * total, axis=0)[:, None]).astype(BF16)

    gathered = lax.all_to_all(
        jnp.broadcast_to(attended[None], (size_x, piece_rows, HEAD_SIZE)), "sx", 0, 0, tiled=True
    )
    gathered = gathered.reshape(CORE_HEADS, z_lo, 2, GROUP, sub, HEAD_SIZE).transpose(2, 0, 1, 4, 3, 5)
    gathered = gathered.reshape(KEY_VALUE_HEADS, z_lo * sub, GROUP * HEAD_SIZE)
    result = jnp.zeros((z_lo * sub, weight.shape[1]), F32)
    for k, block in enumerate(blocks):
        for f in range(2):
            rows = lax.dynamic_index_in_dim(gathered, (sy ^ k) ^ (Y * f), 0, keepdims=False)
            result = result + jnp.dot(rows, block[f], preferred_element_type=F32)
    return result.astype(BF16)


def solution(mesh):
    return jax.shard_map(
        per_device,
        mesh=mesh,
        in_specs=(
            P("sx", None),
            P(("sx", "sy"), None),
            P(("sx", "sy"), None),
            P(),
            P(("sx", "sy")),
            P("sy", "sx"),
        ),
        out_specs=P("sy", "sx"),
        check_vma=False,
    )
```

```python
import jax
import jax.numpy as jnp
from jax import lax
from jax.experimental import pallas as pl
from jax.experimental.pallas import tpu as pltpu
from jax.sharding import PartitionSpec as P

HQ = 40
KEY_VALUE_HEADS = 8
HEAD_SIZE = 128
GROUP = 5
LOG2E = 1.4426950408889634
BF16 = jnp.bfloat16
F32 = jnp.float32
CHIPS = 16
Y = 4
CORE_HEADS = 4
CHUNK = 1024
TILE = 16
PIECE = 2 * GROUP * TILE
STATS = 16
SMALL = 24


def attention_kernel(
    info, valid_pair, q0, q1, q2, q3, key_own, key_pair, value_own, value_pair, out, bias, lhs, factors
):
    head = pl.program_id(0)
    rows = lhs.shape[0]
    tokens = rows // GROUP
    slots = key_own.shape[0]
    tiles = tokens // TILE

    @pl.when(head == 0)
    def _():
        step = 512

        def fill(i, carry):
            start = i * step
            place = lax.broadcasted_iota(jnp.int32, (step, tokens), 0) + start
            token = lax.broadcasted_iota(jnp.int32, (step, tokens), 1)
            pair = place >= slots
            entry = jnp.where(pair, place - slots, place)
            limit = jnp.where(pair, valid_pair[0], info[1])
            base = jnp.where(pair, info[3], info[2])
            seen = (entry < limit) & (base + entry <= token)
            bias[pl.ds(pl.multiple_of(start, step), step), :] = jnp.where(seen, 0.0, -1e30).astype(BF16)
            return carry

        lax.fori_loop(0, 2 * slots // step, fill, 0)
        token = lax.broadcasted_iota(jnp.int32, (tokens, HEAD_SIZE), 0)
        buckets = ((info[4] + token + 1) >> 13).astype(F32)
        scale = (1.0 + 0.1 * jnp.log(buckets + 1.0)) * (HEAD_SIZE ** (-0.5) * LOG2E)
        row = lax.broadcasted_iota(jnp.int32, (TILE, tokens), 0)
        lane = lax.broadcasted_iota(jnp.int32, (TILE, tokens), 1)
        for slot in range(tiles):
            first = ((slot % 2) * Y + slot // 2) * TILE
            one_hot = (lane == row + first).astype(BF16)
            for g in range(GROUP):
                at = slice((slot * GROUP + g) * TILE, (slot * GROUP + g + 1) * TILE)
                lhs[at, HEAD_SIZE:] = one_hot
                factors[at, :] = scale[first : first + TILE]

    for k, block in enumerate((q0, q1, q2, q3)):
        x = info[5 + k]
        for b in range(2):
            slot = ((x % 2) * 2 + b) * 2 + x // 2
            for g in range(GROUP):
                at = pl.multiple_of((slot * GROUP + g) * TILE, TILE)
                lhs[pl.ds(at, TILE), :HEAD_SIZE] = block[
                    b * TILE : (b + 1) * TILE, g * HEAD_SIZE : (g + 1) * HEAD_SIZE
                ]
    left = lhs[...]
    factor = factors[:, :1]
    peak = None
    for source, (keys, values) in enumerate(((key_own, value_own), (key_pair, value_pair))):
        for start in range(0, slots, CHUNK):
            at = slice(source * slots + start, source * slots + start + CHUNK)
            right = jnp.concatenate([keys[start : start + CHUNK, :], bias[at, :]], axis=1)
            scores = lax.dot_general(
                left, right, (((1,), (1,)), ((), ())), preferred_element_type=F32
            )
            top = jnp.max(scores, axis=1, keepdims=True)
            new_peak = top if peak is None else jnp.maximum(peak, top)
            weights = jnp.exp2((scores - new_peak) * factor).astype(BF16)
            both = jnp.concatenate(
                [values[start : start + CHUNK, :], jnp.ones((CHUNK, HEAD_SIZE), BF16)], axis=1
            )
            part = jnp.dot(weights, both, preferred_element_type=F32)
            total = part if peak is None else total * jnp.exp2((peak - new_peak) * factor) + part
            peak = new_peak
    lane = lax.broadcasted_iota(jnp.int32, (rows, HEAD_SIZE), 1)
    rest_m = jnp.broadcast_to(peak * factor, (rows, HEAD_SIZE))
    rest_l = total[:, HEAD_SIZE:]
    packed = jnp.zeros((rows, HEAD_SIZE), F32)
    for k in range(3):
        term_m = rest_m.astype(BF16).astype(F32)
        term_l = rest_l.astype(BF16).astype(F32)
        packed = jnp.where(lane == k, term_m, jnp.where(lane == 3 + k, term_l, packed))
        rest_m, rest_l = rest_m - term_m, rest_l - term_l
    packed = packed.astype(BF16)
    pick = (
        lax.broadcasted_iota(jnp.int32, (8, HEAD_SIZE), 0)
        == lax.broadcasted_iota(jnp.int32, (8, HEAD_SIZE), 1)
    ).astype(BF16)
    for y in range(Y):
        at = slice(y * PIECE, (y + 1) * PIECE)
        out[0, y, :PIECE, :] = total[at, :HEAD_SIZE].astype(BF16)
        turned = lax.dot_general(
            pick, packed[at, :], (((1,), (1,)), ((), ())), preferred_element_type=F32
        )
        second = jnp.concatenate(
            [turned[:, HEAD_SIZE:], jnp.zeros((8, 2 * HEAD_SIZE - PIECE), F32)], axis=1
        )
        out[0, y, PIECE:, :] = jnp.concatenate([turned[:, :HEAD_SIZE], second], axis=0).astype(BF16)


def attend(info, valid_pair, queries, keys, values, key_pair, value_pair):
    tokens = queries[0].shape[0] * 4
    slots = keys.shape[0]
    rows = tokens * GROUP
    cache = pl.BlockSpec((slots, HEAD_SIZE), lambda h, s, v: (0, s[0] * CORE_HEADS + h))
    quarter = pl.BlockSpec((tokens // 4, GROUP * HEAD_SIZE), lambda h, s, v: (0, h))
    return pl.pallas_call(
        attention_kernel,
        grid_spec=pltpu.PrefetchScalarGridSpec(
            num_scalar_prefetch=2,
            grid=(CORE_HEADS,),
            in_specs=[
                quarter,
                quarter,
                quarter,
                quarter,
                cache,
                cache,
                cache,
                cache,
            ],
            out_specs=pl.BlockSpec((1, Y, PIECE + STATS, HEAD_SIZE), lambda h, s, v: (h, 0, 0, 0)),
            scratch_shapes=[
                pltpu.VMEM((2 * slots, tokens), BF16),
                pltpu.VMEM((rows, 2 * HEAD_SIZE), BF16),
                pltpu.VMEM((rows, HEAD_SIZE), F32),
            ],
        ),
        out_shape=jax.ShapeDtypeStruct((CORE_HEADS, Y, PIECE + STATS, HEAD_SIZE), BF16),
        compiler_params=pltpu.CompilerParams(vmem_limit_bytes=60 * 2**20),
        cost_estimate=pl.CostEstimate(
            flops=2 * 2 * CORE_HEADS * rows * 2 * slots * 2 * HEAD_SIZE,
            bytes_accessed=2 * 2 * CORE_HEADS * 2 * slots * HEAD_SIZE,
            transcendentals=CORE_HEADS * rows * 2 * slots,
        ),
    )(info, valid_pair, *queries, keys, key_pair, values, value_pair)


def merge(out, peak, total):
    top = jnp.max(peak, axis=0)
    share = jnp.exp2(peak - top)
    return jnp.sum(out * share[..., None], axis=0), top, jnp.sum(share * total, axis=0)


def per_device(queries, keys, values, opening, valid, weight):
    sx, sy = lax.axis_index("sx"), lax.axis_index("sy")
    size_x, size_y = lax.axis_size("sx"), lax.axis_size("sy")
    core, z_lo, x = sx % 2, (sx // 2) % 4, sx // 8
    own_rows = queries.shape[0]
    tokens = own_rows * size_x
    slots = keys.shape[0]
    half = CORE_HEADS * GROUP * HEAD_SIZE

    def swap(a, axis, bits):
        size = lax.axis_size(axis)
        return lax.ppermute(a, axis, [(i, i ^ bits) for i in range(size)])

    got = swap(queries, "sx", 1)
    chip_rows = jnp.concatenate(
        [jnp.where(core == 0, queries, got), jnp.where(core == 0, got, queries)], axis=0
    )
    chip_rows = lax.dynamic_slice_in_dim(chip_rows, core * half, half, 1)
    chip_rows, keys, values, valid = lax.optimization_barrier((chip_rows, keys, values, valid))
    line = jnp.stack([chip_rows] + [swap(chip_rows, "sx", 2 * k) for k in (1, 2, 3)])
    line = jnp.concatenate(
        [lax.dynamic_index_in_dim(line, z_lo ^ k, 0, keepdims=False) for k in range(4)], axis=0
    )
    line, weight = lax.optimization_barrier((line, weight.T))
    far = swap(weight, "sy", Y)
    all_queries = [line] + [swap(line, "sx", 8 * k) for k in (1, 2, 3)]

    valid_pair = swap(valid, "sx", 1)
    key_pair = swap(keys, "sx", 1)
    value_pair = swap(values, "sx", 1)

    base = (sx * size_y + sy) * slots - opening[0]
    base_pair = ((sx ^ 1) * size_y + sy) * slots - opening[0]
    info = jnp.stack(
        [core, valid[0], base, base_pair, opening[0]] + [x ^ k for k in range(4)]
    ).astype(jnp.int32)
    out = attend(info, valid_pair, all_queries, keys, values, key_pair, value_pair)

    def device(x, z_lo, core, z_hi, y):
        return ((x * 4 + z_lo) * 2 + core) * size_y + z_hi * Y + y

    four, two = range(4), range(2)
    planes = [
        [device(x, z, c, h, y) for x in four for y in four] for z in four for c in two for h in two
    ]
    received = lax.all_to_all(
        out.reshape(CHIPS, PIECE + STATS, HEAD_SIZE),
        ("sx", "sy"), 0, 0, tiled=True, axis_index_groups=planes,
    )
    received, far = lax.optimization_barrier((received, far))
    near = jnp.stack([weight, far])
    near_1, near_3 = swap(near, "sy", 1), swap(near, "sy", 3)
    terms = received[:, PIECE:].astype(F32).reshape(CHIPS, 2, 8, HEAD_SIZE)
    peak = (terms[:, :, 0] + (terms[:, :, 1] + terms[:, :, 2])).reshape(CHIPS, -1)[:, :PIECE]
    total = (terms[:, :, 3] + (terms[:, :, 4] + terms[:, :, 5])).reshape(CHIPS, -1)[:, :PIECE]
    out, peak, total = merge(received[:, :PIECE].astype(F32), peak, total)

    def small(a, fill):
        a = a.reshape((2, PIECE // 2) + a.shape[1:])
        pad = [(0, 0), (0, 4 * SMALL - PIECE // 2)] + [(0, 0)] * (a.ndim - 2)
        a = jnp.pad(a, pad, constant_values=fill)
        return a.reshape((size_y, SMALL) + a.shape[2:])

    stats = jnp.stack([small(peak, 0.0), small(total, 1.0)], axis=1)
    stats = jnp.pad(stats, ((0, 0), (0, 6), (0, HEAD_SIZE - SMALL)))
    lines = [
        [device(x, z, c, h, y) for h in two for z in four] for x in four for c in two for y in four
    ]
    received = lax.all_to_all(
        jnp.concatenate([small(out, 0.0), stats], axis=1),
        ("sx", "sy"), 0, 0, tiled=True, axis_index_groups=lines,
    )
    received, near_1, near_3 = lax.optimization_barrier((received, near_1, near_3))
    blocks = [near, near_1, swap(near_3, "sy", 1), near_3]
    out, _, total = merge(received[:, :SMALL], received[:, SMALL, :SMALL], received[:, SMALL + 1, :SMALL])
    attended = (out / total[:, None]).astype(BF16)

    gathered = lax.all_to_all(
        jnp.broadcast_to(attended[None], (size_x, SMALL, HEAD_SIZE)), "sx", 0, 0, tiled=True
    )
    gathered = gathered.reshape(4, 4, 2, SMALL, HEAD_SIZE).transpose(2, 0, 1, 3, 4)
    gathered = gathered.reshape(KEY_VALUE_HEADS, 4 * SMALL, HEAD_SIZE)[:, : GROUP * TILE]
    gathered = gathered.reshape(KEY_VALUE_HEADS, GROUP, TILE, HEAD_SIZE).transpose(0, 2, 1, 3)
    gathered = gathered.reshape(KEY_VALUE_HEADS, TILE, GROUP * HEAD_SIZE)
    result = jnp.zeros((TILE, weight.shape[0]), F32)
    for k, block in enumerate(blocks):
        for f in range(2):
            rows = lax.dynamic_index_in_dim(gathered, (sy ^ k) ^ (Y * f), 0, keepdims=False)
            result = result + lax.dot_general(
                rows, block[f], (((1,), (1,)), ((), ())), preferred_element_type=F32
            )
    return result.astype(BF16)


def solution(mesh):
    return jax.shard_map(
        per_device,
        mesh=mesh,
        in_specs=(
            P("sx", None),
            P(("sx", "sy"), None),
            P(("sx", "sy"), None),
            P(),
            P(("sx", "sy")),
            P("sy", "sx"),
        ),
        out_specs=P("sy", "sx"),
        check_vma=False,
    )
```

```python
import jax
import jax.numpy as jnp
from jax import lax
from jax.experimental import pallas as pl
from jax.experimental.pallas import tpu as pltpu
from jax.sharding import PartitionSpec as P

HQ = 40
KEY_VALUE_HEADS = 8
HEAD_SIZE = 128
GROUP = 5
LOG2E = 1.4426950408889634
BF16 = jnp.bfloat16
F32 = jnp.float32
CHIPS = 16
Y = 4
CORE_HEADS = 4
CHUNK = 1024
TILE = 16
PIECE = 2 * GROUP * TILE
STATS = 16
SMALL = 24


def attention_kernel(
    info, q0, q1, q2, q3, key_own, key_pair, value_own, value_pair, out, bias, lhs, factors
):
    head = pl.program_id(0)
    rows = lhs.shape[0]
    tokens = rows // GROUP
    slots = key_own.shape[0]
    tiles = tokens // TILE

    @pl.when(head == 0)
    def _():
        step = 256
        token = lax.broadcasted_iota(jnp.int32, (1, tokens), 1)
        for source, (limit, base) in enumerate(((info[1], info[2]), (info[5], info[3]))):
            last = jnp.minimum(limit - 1, token - base)

            def fill(i, carry, source=source, last=last):
                entry = lax.broadcasted_iota(jnp.int32, (step, tokens), 0) + i * step
                at = pl.multiple_of(source * slots + i * step, step)
                bias[pl.ds(at, step), :] = jnp.where(entry <= last, 0.0, -1e30).astype(BF16)
                return carry

            lax.fori_loop(0, slots // step, fill, 0, unroll=True)
        place = lax.broadcasted_iota(jnp.int32, (tokens, HEAD_SIZE), 0)
        buckets = ((info[4] + place + 1) >> 13).astype(F32)
        scale = (1.0 + 0.1 * jnp.log(buckets + 1.0)) * (HEAD_SIZE ** (-0.5) * LOG2E)
        row = lax.broadcasted_iota(jnp.int32, (TILE, tokens), 0)
        lane = lax.broadcasted_iota(jnp.int32, (TILE, tokens), 1)
        for slot in range(tiles):
            first = ((slot % 2) * Y + slot // 2) * TILE
            one_hot = (lane == row + first).astype(BF16)
            for g in range(GROUP):
                at = slice((slot * GROUP + g) * TILE, (slot * GROUP + g + 1) * TILE)
                lhs[at, HEAD_SIZE:] = one_hot
                factors[at, :] = scale[first : first + TILE]

    for k, block in enumerate((q0, q1, q2, q3)):
        x = info[6 + k]
        for b in range(2):
            slot = ((x % 2) * 2 + b) * 2 + x // 2
            for g in range(GROUP):
                at = pl.multiple_of((slot * GROUP + g) * TILE, TILE)
                lhs[pl.ds(at, TILE), :HEAD_SIZE] = block[
                    b * TILE : (b + 1) * TILE, g * HEAD_SIZE : (g + 1) * HEAD_SIZE
                ]
    left = lhs[...]
    factor = factors[:, :1]
    chunks = [
        (keys, values, bias, source * slots, start)
        for source, (keys, values) in enumerate(((key_own, value_own), (key_pair, value_pair)))
        for start in range(0, slots, CHUNK)
    ]

    def score(keys, values, bias, offset, start):
        right = jnp.concatenate(
            [keys[start : start + CHUNK, :], bias[offset + start : offset + start + CHUNK, :]], axis=1
        )
        return lax.dot_general(left, right, (((1,), (1,)), ((), ())), preferred_element_type=F32)

    peak, following = None, score(*chunks[0])
    for i, (_, values, _, _, start) in enumerate(chunks):
        scores = following
        if i + 1 < len(chunks):
            following = score(*chunks[i + 1])
        top = jnp.max(scores, axis=1, keepdims=True)
        new_peak = top if peak is None else jnp.maximum(peak, top)
        weights = jnp.exp2((scores - new_peak) * factor).astype(BF16)
        both = jnp.concatenate(
            [values[start : start + CHUNK, :], jnp.ones((CHUNK, HEAD_SIZE), BF16)], axis=1
        )
        part = jnp.dot(weights, both, preferred_element_type=F32)
        total = part if peak is None else total * jnp.exp2((peak - new_peak) * factor) + part
        peak = new_peak
    lane = lax.broadcasted_iota(jnp.int32, (rows, HEAD_SIZE), 1)
    rest_m = jnp.broadcast_to(peak * factor, (rows, HEAD_SIZE))
    rest_l = total[:, HEAD_SIZE:]
    packed = jnp.zeros((rows, HEAD_SIZE), F32)
    for k in range(3):
        term_m = rest_m.astype(BF16).astype(F32)
        term_l = rest_l.astype(BF16).astype(F32)
        packed = jnp.where(lane == k, term_m, jnp.where(lane == 3 + k, term_l, packed))
        rest_m, rest_l = rest_m - term_m, rest_l - term_l
    packed = packed.astype(BF16)
    pick = (
        lax.broadcasted_iota(jnp.int32, (8, HEAD_SIZE), 0)
        == lax.broadcasted_iota(jnp.int32, (8, HEAD_SIZE), 1)
    ).astype(BF16)
    for y in range(Y):
        at = slice(y * PIECE, (y + 1) * PIECE)
        out[0, y, :PIECE, :] = total[at, :HEAD_SIZE].astype(BF16)
        turned = lax.dot_general(
            pick, packed[at, :], (((1,), (1,)), ((), ())), preferred_element_type=F32
        )
        second = jnp.concatenate(
            [turned[:, HEAD_SIZE:], jnp.zeros((8, 2 * HEAD_SIZE - PIECE), F32)], axis=1
        )
        out[0, y, PIECE:, :] = jnp.concatenate([turned[:, :HEAD_SIZE], second], axis=0).astype(BF16)


def attend(info, queries, keys, values, key_pair, value_pair):
    tokens = queries[0].shape[0] * 4
    slots = keys.shape[0]
    rows = tokens * GROUP
    cache = pl.BlockSpec((slots, HEAD_SIZE), lambda h, s: (0, s[0] * CORE_HEADS + h))
    quarter = pl.BlockSpec((tokens // 4, GROUP * HEAD_SIZE), lambda h, s: (0, h))
    return pl.pallas_call(
        attention_kernel,
        grid_spec=pltpu.PrefetchScalarGridSpec(
            num_scalar_prefetch=1,
            grid=(CORE_HEADS,),
            in_specs=[
                quarter,
                quarter,
                quarter,
                quarter,
                cache,
                cache,
                cache,
                cache,
            ],
            out_specs=pl.BlockSpec((1, Y, PIECE + STATS, HEAD_SIZE), lambda h, s: (h, 0, 0, 0)),
            scratch_shapes=[
                pltpu.VMEM((2 * slots, tokens), BF16),
                pltpu.VMEM((rows, 2 * HEAD_SIZE), BF16),
                pltpu.VMEM((rows, HEAD_SIZE), F32),
            ],
        ),
        out_shape=jax.ShapeDtypeStruct((CORE_HEADS, Y, PIECE + STATS, HEAD_SIZE), BF16),
        compiler_params=pltpu.CompilerParams(vmem_limit_bytes=60 * 2**20),
        cost_estimate=pl.CostEstimate(
            flops=2 * 2 * CORE_HEADS * rows * 2 * slots * 2 * HEAD_SIZE,
            bytes_accessed=2 * 2 * CORE_HEADS * 2 * slots * HEAD_SIZE,
            transcendentals=CORE_HEADS * rows * 2 * slots,
        ),
    )(info, *queries, keys, key_pair, values, value_pair)


def merge(out, peak, total):
    top = jnp.max(peak, axis=0)
    share = jnp.exp2(peak - top)
    return jnp.sum(out * share[..., None], axis=0), top, jnp.sum(share * total, axis=0)


def per_device(queries, keys, values, opening, valid, weight):
    sx, sy = lax.axis_index("sx"), lax.axis_index("sy")
    size_x, size_y = lax.axis_size("sx"), lax.axis_size("sy")
    core, z_lo, x = sx % 2, (sx // 2) % 4, sx // 8
    own_rows = queries.shape[0]
    tokens = own_rows * size_x
    slots = keys.shape[0]
    half = CORE_HEADS * GROUP * HEAD_SIZE

    def swap(a, axis, bits):
        size = lax.axis_size(axis)
        return lax.ppermute(a, axis, [(i, i ^ bits) for i in range(size)])

    got = swap(queries, "sx", 1)
    chip_rows = jnp.concatenate(
        [jnp.where(core == 0, queries, got), jnp.where(core == 0, got, queries)], axis=0
    )
    chip_rows = lax.dynamic_slice_in_dim(chip_rows, core * half, half, 1)
    valid_pair = swap(valid, "sx", 1)
    chip_rows, keys, values, valid_pair = lax.optimization_barrier((chip_rows, keys, values, valid_pair))
    line = jnp.stack([chip_rows] + [swap(chip_rows, "sx", 2 * k) for k in (1, 2, 3)])
    line = jnp.concatenate(
        [lax.dynamic_index_in_dim(line, z_lo ^ k, 0, keepdims=False) for k in range(4)], axis=0
    )
    line, weight = lax.optimization_barrier((line, weight.T))
    far = swap(weight, "sy", Y)
    all_queries = [line] + [swap(line, "sx", 8 * k) for k in (1, 2, 3)]

    key_pair = swap(keys, "sx", 1)
    value_pair = swap(values, "sx", 1)

    base = (sx * size_y + sy) * slots - opening[0]
    base_pair = ((sx ^ 1) * size_y + sy) * slots - opening[0]
    info = jnp.stack(
        [core, valid[0], base, base_pair, opening[0], valid_pair[0]] + [x ^ k for k in range(4)]
    ).astype(jnp.int32)
    out = attend(info, all_queries, keys, values, key_pair, value_pair)
    out, far = lax.optimization_barrier((out, far))

    def device(x, z_lo, core, z_hi, y):
        return ((x * 4 + z_lo) * 2 + core) * size_y + z_hi * Y + y

    four, two = range(4), range(2)
    planes = [
        [device(x, z, c, h, y) for x in four for y in four] for z in four for c in two for h in two
    ]
    received = lax.all_to_all(
        out.reshape(CHIPS, PIECE + STATS, HEAD_SIZE),
        ("sx", "sy"), 0, 0, tiled=True, axis_index_groups=planes,
    )
    received, far = lax.optimization_barrier((received, far))
    near = jnp.stack([weight, far])
    near_1, near_3 = swap(near, "sy", 1), swap(near, "sy", 3)
    terms = received[:, PIECE:].astype(F32).reshape(CHIPS, 2, 8, HEAD_SIZE)
    peak = (terms[:, :, 0] + (terms[:, :, 1] + terms[:, :, 2])).reshape(CHIPS, -1)[:, :PIECE]
    total = (terms[:, :, 3] + (terms[:, :, 4] + terms[:, :, 5])).reshape(CHIPS, -1)[:, :PIECE]
    out, peak, total = merge(received[:, :PIECE].astype(F32), peak, total)

    rows = PIECE // 2

    def wide(a):
        return jnp.pad(a.reshape(2, 1, rows), ((0, 0), (0, 0), (0, HEAD_SIZE - rows)))

    stats = jnp.concatenate([wide(peak), wide(total), jnp.zeros((2, 6, HEAD_SIZE), F32)], axis=1)
    pieces = jnp.concatenate([out.reshape(2, rows, HEAD_SIZE), stats], axis=1)
    pieces = jnp.broadcast_to(pieces[:, None], (2, 4, rows + 8, HEAD_SIZE))
    lines = [
        [device(x, z, c, h, y) for h in two for z in four] for x in four for c in two for y in four
    ]
    received = lax.all_to_all(
        pieces.reshape(size_y, rows + 8, HEAD_SIZE),
        ("sx", "sy"), 0, 0, tiled=True, axis_index_groups=lines,
    )
    received, near_1, near_3 = lax.optimization_barrier((received, near_1, near_3))
    near_2 = [swap(near_1[0], "sy", 3), swap(near_3[1], "sy", 1)]
    blocks = [near, near_1, near_2, near_3]
    out, _, total = merge(received[:, :rows], received[:, rows, :rows], received[:, rows + 1, :rows])
    attended = (out / total[:, None]).astype(BF16)

    got = swap(attended, "sx", 1)
    both = jnp.stack([jnp.where(core == 0, attended, got), jnp.where(core == 0, got, attended)])
    rings = [[(i * 4 + z) * 2 + c for i in four] for z in four for c in two]
    gathered = lax.all_to_all(
        jnp.broadcast_to(both[None], (4, 2, rows, HEAD_SIZE)), "sx", 0, 0, tiled=True, axis_index_groups=rings
    )
    gathered = gathered.reshape(4, 2, GROUP, TILE, HEAD_SIZE).transpose(1, 0, 3, 2, 4)
    gathered = gathered.reshape(KEY_VALUE_HEADS, TILE, GROUP * HEAD_SIZE)
    result = jnp.zeros((TILE, weight.shape[0]), F32)
    for k, block in enumerate(blocks):
        for f in range(2):
            left = lax.dynamic_index_in_dim(gathered, (sy ^ k) ^ (Y * f), 0, keepdims=False)
            result = result + lax.dot_general(
                left, block[f], (((1,), (1,)), ((), ())), preferred_element_type=F32
            )
    return result.astype(BF16)


def solution(mesh):
    return jax.shard_map(
        per_device,
        mesh=mesh,
        in_specs=(
            P("sx", None),
            P(("sx", "sy"), None),
            P(("sx", "sy"), None),
            P(),
            P(("sx", "sy")),
            P("sy", "sx"),
        ),
        out_specs=P("sy", "sx"),
        check_vma=False,
    )
```

```python
import jax
import jax.numpy as jnp
from jax import lax
from jax.experimental import pallas as pl
from jax.experimental.pallas import tpu as pltpu
from jax.sharding import PartitionSpec as P

HQ = 40
KEY_VALUE_HEADS = 8
HEAD_SIZE = 128
GROUP = 5
LOG2E = 1.4426950408889634
BF16 = jnp.bfloat16
F32 = jnp.float32
CHIPS = 16
Y = 4
CORE_HEADS = 4
CHUNK = 2048
TILE = 16
PIECE = 2 * GROUP * TILE
STATS = 16
SMALL = 24


def attention_kernel(
    info, q0, q1, q2, q3, key_own, key_pair, value_own, value_pair, out, bias, lhs, factors
):
    head = pl.program_id(0)
    rows = lhs.shape[0]
    tokens = rows // GROUP
    slots = key_own.shape[0]
    tiles = tokens // TILE

    @pl.when(head == 0)
    def _():
        step = 256
        token = lax.broadcasted_iota(jnp.int32, (1, tokens), 1)
        for source, (limit, base) in enumerate(((info[1], info[2]), (info[5], info[3]))):
            last = jnp.minimum(limit - 1, token - base)

            def fill(i, carry, source=source, last=last):
                entry = lax.broadcasted_iota(jnp.int32, (step, tokens), 0) + i * step
                at = pl.multiple_of(source * slots + i * step, step)
                bias[pl.ds(at, step), :] = jnp.where(entry <= last, 0.0, -1e30).astype(BF16)
                return carry

            lax.fori_loop(0, slots // step, fill, 0, unroll=True)
        place = lax.broadcasted_iota(jnp.int32, (tokens, HEAD_SIZE), 0)
        buckets = ((info[4] + place + 1) >> 13).astype(F32)
        scale = (1.0 + 0.1 * jnp.log(buckets + 1.0)) * (HEAD_SIZE ** (-0.5) * LOG2E)
        row = lax.broadcasted_iota(jnp.int32, (TILE, tokens), 0)
        lane = lax.broadcasted_iota(jnp.int32, (TILE, tokens), 1)
        for slot in range(tiles):
            first = ((slot % 2) * Y + slot // 2) * TILE
            one_hot = (lane == row + first).astype(BF16)
            for g in range(GROUP):
                at = slice((slot * GROUP + g) * TILE, (slot * GROUP + g + 1) * TILE)
                lhs[at, HEAD_SIZE:] = one_hot
                factors[at, :] = scale[first : first + TILE]

    for k, block in enumerate((q0, q1, q2, q3)):
        x = info[6 + k]
        for b in range(2):
            slot = ((x % 2) * 2 + b) * 2 + x // 2
            for g in range(GROUP):
                at = pl.multiple_of((slot * GROUP + g) * TILE, TILE)
                lhs[pl.ds(at, TILE), :HEAD_SIZE] = block[
                    b * TILE : (b + 1) * TILE, g * HEAD_SIZE : (g + 1) * HEAD_SIZE
                ]
    left = lhs[...]
    factor = factors[:, :1]
    chunks = [
        (keys, values, bias, source * slots, start)
        for source, (keys, values) in enumerate(((key_own, value_own), (key_pair, value_pair)))
        for start in range(0, slots, CHUNK)
    ]

    def score(keys, values, bias, offset, start):
        right = jnp.concatenate(
            [keys[start : start + CHUNK, :], bias[offset + start : offset + start + CHUNK, :]], axis=1
        )
        return lax.dot_general(left, right, (((1,), (1,)), ((), ())), preferred_element_type=F32)

    peak, following = None, score(*chunks[0])
    for i, (_, values, _, _, start) in enumerate(chunks):
        scores = following
        if i + 1 < len(chunks):
            following = score(*chunks[i + 1])
        top = jnp.max(scores, axis=1, keepdims=True)
        new_peak = top if peak is None else jnp.maximum(peak, top)
        weights = jnp.exp2((scores - new_peak) * factor).astype(BF16)
        both = jnp.concatenate(
            [values[start : start + CHUNK, :], jnp.ones((CHUNK, HEAD_SIZE), BF16)], axis=1
        )
        part = jnp.dot(weights, both, preferred_element_type=F32)
        total = part if peak is None else total * jnp.exp2((peak - new_peak) * factor) + part
        peak = new_peak
    lane = lax.broadcasted_iota(jnp.int32, (rows, HEAD_SIZE), 1)
    rest_m = jnp.broadcast_to(peak * factor, (rows, HEAD_SIZE))
    rest_l = total[:, HEAD_SIZE:]
    packed = jnp.zeros((rows, HEAD_SIZE), F32)
    for k in range(3):
        term_m = rest_m.astype(BF16).astype(F32)
        term_l = rest_l.astype(BF16).astype(F32)
        packed = jnp.where(lane == k, term_m, jnp.where(lane == 3 + k, term_l, packed))
        rest_m, rest_l = rest_m - term_m, rest_l - term_l
    packed = packed.astype(BF16)
    pick = (
        lax.broadcasted_iota(jnp.int32, (8, HEAD_SIZE), 0)
        == lax.broadcasted_iota(jnp.int32, (8, HEAD_SIZE), 1)
    ).astype(BF16)
    for y in range(Y):
        at = slice(y * PIECE, (y + 1) * PIECE)
        out[0, y, :PIECE, :] = total[at, :HEAD_SIZE].astype(BF16)
        turned = lax.dot_general(
            pick, packed[at, :], (((1,), (1,)), ((), ())), preferred_element_type=F32
        )
        second = jnp.concatenate(
            [turned[:, HEAD_SIZE:], jnp.zeros((8, 2 * HEAD_SIZE - PIECE), F32)], axis=1
        )
        out[0, y, PIECE:, :] = jnp.concatenate([turned[:, :HEAD_SIZE], second], axis=0).astype(BF16)


def attend(info, queries, keys, values, key_pair, value_pair):
    tokens = queries[0].shape[0] * 4
    slots = keys.shape[0]
    rows = tokens * GROUP
    cache = pl.BlockSpec((slots, HEAD_SIZE), lambda h, s: (0, s[0] * CORE_HEADS + h))
    quarter = pl.BlockSpec((tokens // 4, GROUP * HEAD_SIZE), lambda h, s: (0, h))
    return pl.pallas_call(
        attention_kernel,
        grid_spec=pltpu.PrefetchScalarGridSpec(
            num_scalar_prefetch=1,
            grid=(CORE_HEADS,),
            in_specs=[
                quarter,
                quarter,
                quarter,
                quarter,
                cache,
                cache,
                cache,
                cache,
            ],
            out_specs=pl.BlockSpec((1, Y, PIECE + STATS, HEAD_SIZE), lambda h, s: (h, 0, 0, 0)),
            scratch_shapes=[
                pltpu.VMEM((2 * slots, tokens), BF16),
                pltpu.VMEM((rows, 2 * HEAD_SIZE), BF16),
                pltpu.VMEM((rows, HEAD_SIZE), F32),
            ],
        ),
        out_shape=jax.ShapeDtypeStruct((CORE_HEADS, Y, PIECE + STATS, HEAD_SIZE), BF16),
        compiler_params=pltpu.CompilerParams(vmem_limit_bytes=60 * 2**20),
        cost_estimate=pl.CostEstimate(
            flops=2 * 2 * CORE_HEADS * rows * 2 * slots * 2 * HEAD_SIZE,
            bytes_accessed=2 * 2 * CORE_HEADS * 2 * slots * HEAD_SIZE,
            transcendentals=CORE_HEADS * rows * 2 * slots,
        ),
    )(info, *queries, keys, key_pair, values, value_pair)


def merge(out, peak, total):
    top = jnp.max(peak, axis=0)
    share = jnp.exp2(peak - top)
    return jnp.sum(out * share[..., None], axis=0), top, jnp.sum(share * total, axis=0)


def per_device(queries, keys, values, opening, valid, weight):
    sx, sy = lax.axis_index("sx"), lax.axis_index("sy")
    size_x, size_y = lax.axis_size("sx"), lax.axis_size("sy")
    core, z_lo, x = sx % 2, (sx // 2) % 4, sx // 8
    own_rows = queries.shape[0]
    tokens = own_rows * size_x
    slots = keys.shape[0]
    half = CORE_HEADS * GROUP * HEAD_SIZE

    def swap(a, axis, bits):
        size = lax.axis_size(axis)
        return lax.ppermute(a, axis, [(i, i ^ bits) for i in range(size)])

    got = swap(queries, "sx", 1)
    chip_rows = jnp.concatenate(
        [jnp.where(core == 0, queries, got), jnp.where(core == 0, got, queries)], axis=0
    )
    chip_rows = lax.dynamic_slice_in_dim(chip_rows, core * half, half, 1)
    valid_pair = swap(valid, "sx", 1)
    chip_rows, keys, values, valid_pair = lax.optimization_barrier((chip_rows, keys, values, valid_pair))
    line = jnp.stack([chip_rows] + [swap(chip_rows, "sx", 2 * k) for k in (1, 2, 3)])
    line = jnp.concatenate(
        [lax.dynamic_index_in_dim(line, z_lo ^ k, 0, keepdims=False) for k in range(4)], axis=0
    )
    line, weight = lax.optimization_barrier((line, weight.T))
    far = swap(weight, "sy", Y)
    all_queries = [line] + [swap(line, "sx", 8 * k) for k in (1, 2, 3)]

    key_pair = swap(keys, "sx", 1)
    value_pair = swap(values, "sx", 1)

    base = (sx * size_y + sy) * slots - opening[0]
    base_pair = ((sx ^ 1) * size_y + sy) * slots - opening[0]
    info = jnp.stack(
        [core, valid[0], base, base_pair, opening[0], valid_pair[0]] + [x ^ k for k in range(4)]
    ).astype(jnp.int32)
    out = attend(info, all_queries, keys, values, key_pair, value_pair)
    out, far = lax.optimization_barrier((out, far))

    def device(x, z_lo, core, z_hi, y):
        return ((x * 4 + z_lo) * 2 + core) * size_y + z_hi * Y + y

    four, two = range(4), range(2)
    planes = [
        [device(x, z, c, h, y) for x in four for y in four] for z in four for c in two for h in two
    ]
    received = lax.all_to_all(
        out.reshape(CHIPS, PIECE + STATS, HEAD_SIZE),
        ("sx", "sy"), 0, 0, tiled=True, axis_index_groups=planes,
    )
    received, far = lax.optimization_barrier((received, far))
    near = jnp.stack([weight, far])
    near_1, near_3 = swap(near, "sy", 1), swap(near, "sy", 3)
    terms = received[:, PIECE:].astype(F32).reshape(CHIPS, 2, 8, HEAD_SIZE)
    peak = (terms[:, :, 0] + (terms[:, :, 1] + terms[:, :, 2])).reshape(CHIPS, -1)[:, :PIECE]
    total = (terms[:, :, 3] + (terms[:, :, 4] + terms[:, :, 5])).reshape(CHIPS, -1)[:, :PIECE]
    out, peak, total = merge(received[:, :PIECE].astype(F32), peak, total)

    rows = PIECE // 2

    def wide(a):
        return jnp.pad(a.reshape(2, 1, rows), ((0, 0), (0, 0), (0, HEAD_SIZE - rows)))

    stats = jnp.concatenate([wide(peak), wide(total), jnp.zeros((2, 6, HEAD_SIZE), F32)], axis=1)
    pieces = jnp.concatenate([out.reshape(2, rows, HEAD_SIZE), stats], axis=1)
    pieces = jnp.broadcast_to(pieces[:, None], (2, 4, rows + 8, HEAD_SIZE))
    lines = [
        [device(x, z, c, h, y) for h in two for z in four] for x in four for c in two for y in four
    ]
    received = lax.all_to_all(
        pieces.reshape(size_y, rows + 8, HEAD_SIZE),
        ("sx", "sy"), 0, 0, tiled=True, axis_index_groups=lines,
    )
    received, near_1, near_3 = lax.optimization_barrier((received, near_1, near_3))
    near_2 = [swap(near_1[0], "sy", 3), swap(near_3[1], "sy", 1)]
    blocks = [near, near_1, near_2, near_3]
    out, _, total = merge(received[:, :rows], received[:, rows, :rows], received[:, rows + 1, :rows])
    attended = (out / total[:, None]).astype(BF16)

    got = swap(attended, "sx", 1)
    both = jnp.stack([jnp.where(core == 0, attended, got), jnp.where(core == 0, got, attended)])
    rings = [[(i * 4 + z) * 2 + c for i in four] for z in four for c in two]
    gathered = lax.all_to_all(
        jnp.broadcast_to(both[None], (4, 2, rows, HEAD_SIZE)), "sx", 0, 0, tiled=True, axis_index_groups=rings
    )
    gathered = gathered.reshape(4, 2, GROUP, TILE, HEAD_SIZE).transpose(1, 0, 3, 2, 4)
    gathered = gathered.reshape(KEY_VALUE_HEADS, TILE, GROUP * HEAD_SIZE)
    result = jnp.zeros((TILE, weight.shape[0]), F32)
    for k, block in enumerate(blocks):
        for f in range(2):
            left = lax.dynamic_index_in_dim(gathered, (sy ^ k) ^ (Y * f), 0, keepdims=False)
            result = result + lax.dot_general(
                left, block[f], (((1,), (1,)), ((), ())), preferred_element_type=F32
            )
    return result.astype(BF16)


def solution(mesh):
    return jax.shard_map(
        per_device,
        mesh=mesh,
        in_specs=(
            P("sx", None),
            P(("sx", "sy"), None),
            P(("sx", "sy"), None),
            P(),
            P(("sx", "sy")),
            P("sy", "sx"),
        ),
        out_specs=P("sy", "sx"),
        check_vma=False,
    )
```
